32 devices in a mesh: row: 2 (over core), circ: 4 (over z), rad: 4 (over y, x).
Axes of the slice: x: 2, y: 2, z: 4, core: 2. Of those that a mesh axis runs over, the one named last changes fastest.
Arguments:
- flow: float32 [2, 5, 8, 32, 512], P('row', None, None, 'rad', 'circ'), may hold values from -2 to 8, as said below
- inflow: float32 [5, 32, 512], P(None, 'rad', 'circ'), may hold values from -2 to 8, as said below
- outflow: float32 [5, 32, 512], P(None, 'rad', 'circ'), may hold values from -2 to 8, as said below
- wheel: float32 [32], P('rad'), may hold values from 0.3 to 0.7
- offsets: int32 [2], replicated, may hold values from 0 to 511
Outputs:
- advanced: float32 [2, 5, 8, 32, 512], P('row', None, None, 'rad', 'circ')
The draws below stay inside these ranges and needn't reach their ends.
Inputs may be any that keep to these rules, and one draw needn't show every extreme that they name: Physical states: density positive, pressure positive, flow mainly axial. `inflow`: physical states, like flow. `outflow`: physical states, like flow.
All inputs are finite; a program needn't handle non-finite values.
Results may differ from the reference program's by a relative error of at most 0.00002.
Values sent between devices are 32-bit elements; how exact they have to be, the bound alone decides.
A program may use at most 64 MiB of HBM per device.

```python
import jax
import jax.numpy as jnp

CA = 8
STEPS = 2
NRAD = 32
NTH = 512


GAMMA = 1.4


def physical_state(key, lead_shape, stack_axis):
    subkeys = jax.random.split(key, 5)
    density = 1.0 + 0.15 * jax.random.truncated_normal(subkeys[0], -2.0, 2.0, lead_shape, jnp.float32)
    axial = 0.5 + 0.1 * jax.random.truncated_normal(subkeys[1], -2.0, 2.0, lead_shape, jnp.float32)
    radial = 0.08 * jax.random.truncated_normal(subkeys[2], -2.0, 2.0, lead_shape, jnp.float32)
    swirl = 0.1 * jax.random.truncated_normal(subkeys[3], -2.0, 2.0, lead_shape, jnp.float32)
    pressure = 1.0 + 0.15 * jax.random.truncated_normal(subkeys[4], -2.0, 2.0, lead_shape, jnp.float32)
    energy = pressure / (GAMMA - 1.0) + 0.5 * density * (axial * axial + radial * radial + swirl * swirl)
    return jnp.stack([density, density * axial, density * radial, density * swirl, energy], axis=stack_axis)


def draw_flow(key, part):
    return physical_state(jax.random.fold_in(key, 11), (2, CA, NRAD, NTH), 1)


def draw_inflow(key, part):
    return physical_state(jax.random.fold_in(key, 23), (NRAD, NTH), 0)


def draw_outflow(key, part):
    return physical_state(jax.random.fold_in(key, 37), (NRAD, NTH), 0)


def steps_of(stream_key, extent, cuts, least, top_value):
    gain, own = 1.0, jax.random.fold_in(stream_key, 6)
    for axis_at, parts in cuts:
        draws = jnp.exp(jax.random.uniform(jax.random.fold_in(own, axis_at), (parts,), jnp.float32, least / len(cuts), top_value / len(cuts)))
        gain = gain * jnp.repeat(draws, extent[axis_at] // parts).reshape([-1 if axis == axis_at else 1 for axis in range(len(extent))])
    return gain


def setup_inputs(seed: int = 0) -> dict:
    key_list = jax.random.split(jax.random.key(seed), 6)
    flow = draw_flow(jax.random.fold_in(key_list[5], 71), 0)
    inflow = draw_inflow(jax.random.fold_in(key_list[5], 71), 0)
    outflow = draw_outflow(jax.random.fold_in(key_list[5], 71), 0)
    wheel = jnp.clip(0.3 + 0.39999998 * jax.random.uniform(key_list[3], (NRAD,), jnp.float32) ** steps_of(key_list[3], (NRAD,), ((0, 4),), -0.2, 0.2), 0.3, 0.7)
    offsets = jax.random.randint(key_list[4], (STEPS,), 0, NTH).astype(jnp.int32)
    return dict(flow=flow, inflow=inflow, outflow=outflow, wheel=wheel, offsets=offsets)


GAMMA = 1.4
COURANT = 0.1

def unit_vector(index):
    values = [0.0, 0.0, 0.0, 0.0, 0.0]
    values[index] = 1.0
    return jnp.array(values, dtype=jnp.float32).reshape(5, 1, 1, 1)

def physical_flux(field, normal_axis):
    density = field[0]
    inverse = 1.0 / density
    velocity = field[1:4] * inverse
    kinetic = 0.5 * (field[1] * velocity[0] + field[2] * velocity[1] + field[3] * velocity[2])
    pressure = (GAMMA - 1.0) * (field[4] - kinetic)
    normal_vel = velocity[normal_axis]
    flux_terms = field * normal_vel + pressure * unit_vector(1 + normal_axis) + pressure * normal_vel * unit_vector(4)
    wave_speed = jnp.abs(normal_vel) + jnp.sqrt(GAMMA * pressure / density)
    return (flux_terms, wave_speed)

def face_flux(left_cells, right_cells, normal_axis):
    flux_left, speed_left = physical_flux(left_cells, normal_axis)
    flux_right, speed_right = physical_flux(right_cells, normal_axis)
    return 0.5 * (flux_left + flux_right) - 0.5 * jnp.maximum(speed_left, speed_right) * (right_cells - left_cells)

def divergence(axial_pad, radial_pad, circ_pad):
    flux_axial = face_flux(axial_pad[:, :-1], axial_pad[:, 1:], 0)
    flux_radial = face_flux(radial_pad[:, :, :-1], radial_pad[:, :, 1:], 1)
    flux_circ = face_flux(circ_pad[..., :-1], circ_pad[..., 1:], 2)
    total = flux_axial[:, 1:] - flux_axial[:, :-1] + (flux_radial[:, :, 1:] - flux_radial[:, :, :-1]) + (flux_circ[..., 1:] - flux_circ[..., :-1])
    return -COURANT * total

def mirrored(layer):
    signs = jnp.array([1.0, 1.0, -1.0, 1.0, 1.0], dtype=jnp.float32).reshape(5, 1, 1, 1)
    return layer * signs

def reframe(layer, wheel, direction_sign):
    density = layer[0]
    swirl = layer[3]
    blade = wheel[:, None]
    new_swirl = swirl + direction_sign * density * blade
    new_energy = layer[4] + direction_sign * swirl * blade + 0.5 * density * blade * blade
    return jnp.stack([layer[0], layer[1], layer[2], new_swirl, new_energy])

def row_change(field, lower_face, upper_face):
    axial_pad = jnp.concatenate([lower_face[:, None], field, upper_face[:, None]], axis=1)
    radial_pad = jnp.concatenate([mirrored(field[:, :, :1]), field, mirrored(field[:, :, -1:])], axis=2)
    circ_pad = jnp.concatenate([field[..., -1:], field, field[..., :1]], axis=3)
    return divergence(axial_pad, radial_pad, circ_pad)

def both_changes(rotor, stator, offset_now, inflow, outflow, wheel):
    rotor_ghost = reframe(jnp.roll(stator[:, 0], -offset_now, axis=-1), wheel, -1.0)
    stator_ghost = reframe(jnp.roll(rotor[:, -1], offset_now, axis=-1), wheel, 1.0)
    return (row_change(rotor, inflow, rotor_ghost), row_change(stator, stator_ghost, outflow))

def reference(flow, inflow, outflow, wheel, offsets):
    rotor = flow[0]
    stator = flow[1]
    for step in range(STEPS):
        offset_now = offsets[step]
        change_r, change_s = both_changes(rotor, stator, offset_now, inflow, outflow, wheel)
        first_r = rotor + change_r
        first_s = stator + change_s
        change_r, change_s = both_changes(first_r, first_s, offset_now, inflow, outflow, wheel)
        second_r = 0.75 * rotor + 0.25 * (first_r + change_r)
        second_s = 0.75 * stator + 0.25 * (first_s + change_s)
        change_r, change_s = both_changes(second_r, second_s, offset_now, inflow, outflow, wheel)
        rotor = rotor / 3.0 + 2.0 / 3.0 * (second_r + change_r)
        stator = stator / 3.0 + 2.0 / 3.0 * (second_s + change_s)
    return jnp.stack([rotor, stator])
```

```python
import functools

import jax
import jax.numpy as jnp
from jax import lax
from jax.experimental import pallas as pl
from jax.experimental.pallas import tpu as pltpu
from jax.sharding import PartitionSpec as P

GAMMA = 1.4
COURANT = 0.1
MESH = pl.DeviceIdType.MESH
STAGES = 3


def primitives(q):
    inverse = 1.0 / q[0]
    vel = [q[1] * inverse, q[2] * inverse, q[3] * inverse]
    kinetic = 0.5 * (q[1] * vel[0] + q[2] * vel[1] + q[3] * vel[2])
    pressure = (GAMMA - 1.0) * (q[4] - kinetic)
    sound = jnp.sqrt(GAMMA * pressure * inverse)
    return vel, pressure, sound


def normal_flux(q, prim, k):
    vel, pressure, sound = prim
    v = vel[k]
    f = [q[1 + k], q[1] * v, q[2] * v, q[3] * v, (q[4] + pressure) * v]
    f[1 + k] = f[1 + k] + pressure
    return f, jnp.abs(v) + sound


def jump(speed_a, speed_b, left, right):
    s = jnp.maximum(speed_a, speed_b)
    return [s * (right[c] - left[c]) for c in range(5)]


def kernel(
    nc, nr, steps,
    flow_ref, inflow_ref, outflow_ref, wheel_ref, offsets_ref,
    out_ref,
    state, far, gsend, grecv, csend, crecv, rsend, rrecv,
    gs_sem, gr_sem, hs_sem, hr_sem,
):
    ca, rows, cols = state.shape[2:]
    total = steps * STAGES
    row = lax.axis_index("row")
    me = lax.axis_index("circ")
    rad = lax.axis_index("rad")
    is_rotor = row == 0
    other = 1 - row
    right, left = lax.rem(me + 1, nc), lax.rem(me + nc - 1, nc)
    above, below = lax.rem(rad + 1, nr), lax.rem(rad + nr - 1, nr)

    barrier = pltpu.get_barrier_semaphore()
    for d in range(nc):
        pl.semaphore_signal(
            barrier, inc=1, device_id=(other, lax.rem(me + d, nc), rad), device_id_type=MESH)
    for peer in ((row, right, rad), (row, left, rad), (row, me, above), (row, me, below)):
        pl.semaphore_signal(barrier, inc=1, device_id=peer, device_id_type=MESH)

    lane = lax.broadcasted_iota(jnp.int32, (rows, cols), 1)
    sub = lax.broadcasted_iota(jnp.int32, (rows, cols), 0)
    first_lane, last_lane = lane == 0, lane == cols - 1
    first_sub, last_sub = sub == 0, sub == rows - 1
    wall_lo = jnp.logical_and(first_sub, rad == 0)
    wall_hi = jnp.logical_and(last_sub, rad == nr - 1)
    pair = lax.div(lane, 2)
    even = lax.rem(lane, 2) == 0
    sigma = jnp.where(is_rotor, jnp.float32(-1.0), jnp.float32(1.0))
    blade = jnp.zeros((rows, cols), jnp.float32)
    for r in range(rows):
        blade = jnp.where(sub == r, wheel_ref[r], blade)

    def axial(k):
        return jnp.where(is_rotor, ca - 1 - k, k)

    def gather_copy(slot, d):
        return pltpu.make_async_remote_copy(
            src_ref=gsend.at[slot], dst_ref=grecv.at[slot, me],
            send_sem=gs_sem.at[slot, d], recv_sem=gr_sem.at[slot, me],
            device_id=(other, lax.rem(me + d, nc), rad), device_id_type=MESH)

    def gather_arrival(slot, j):
        return pltpu.make_async_remote_copy(
            src_ref=gsend.at[slot], dst_ref=grecv.at[slot, j],
            send_sem=gs_sem.at[slot, j], recv_sem=gr_sem.at[slot, j],
            device_id=(other, me, rad), device_id_type=MESH)

    def halo_copies(slot):
        plan = (
            (csend.at[slot], crecv.at[slot, 0], (row, right, rad)),
            (csend.at[slot], crecv.at[slot, 1], (row, left, rad)),
            (rsend.at[slot, 0], rrecv.at[slot, 0], (row, me, above)),
            (rsend.at[slot, 1], rrecv.at[slot, 1], (row, me, below)),
        )
        return [
            pltpu.make_async_remote_copy(
                src_ref=src, dst_ref=dst, send_sem=hs_sem.at[slot, i],
                recv_sem=hr_sem.at[slot, i], device_id=peer, device_id_type=MESH)
            for i, (src, dst, peer) in enumerate(plan)
        ]

    order = sorted(range(nc), key=lambda d: -min(d, nc - d))

    def start_gather(slot):
        for d in order:
            gather_copy(slot, d).start()

    def pack(slot, k, q, packed):
        for c in range(5):
            rsend[slot, 0, c, k : k + 1, :] = q[c][rows - 1 : rows, :]
            rsend[slot, 1, c, k : k + 1, :] = q[c][0:1, :]
            place = c * ca + k
            packed = jnp.where(pair == place, pltpu.roll(q[c], 2 * place + 1, 1), packed)
        return packed

    zero = jnp.zeros((rows, cols), jnp.float32)
    packed = zero
    for c in range(5):
        far[c] = jnp.where(is_rotor, inflow_ref[c], outflow_ref[c])
    for k in range(ca):
        q = [flow_ref[0, c, axial(k)] for c in range(5)]
        for c in range(5):
            state[0, c, k] = q[c]
            if k == 0:
                gsend[0, c] = q[c]
        packed = pack(0, k, q, packed)
    csend[0] = packed
    pl.semaphore_wait(barrier, nc + 4)
    start_gather(0)
    for copy in halo_copies(0):
        copy.start()

    def stage(s, carry):
        step = lax.div(s, STAGES)
        phase = s - step * STAGES
        base = step * STAGES
        keep = jnp.where(phase == 0, 0.0, jnp.where(phase == 1, 0.75, 1.0 / 3.0)).astype(jnp.float32)
        mix = jnp.where(phase == 0, 1.0, jnp.where(phase == 1, 0.25, 2.0 / 3.0)).astype(jnp.float32)

        for copy in halo_copies(s):
            copy.wait_recv()
        merged = jnp.where(
            even, pltpu.roll(crecv[s, 1], cols - 1, 1), pltpu.roll(crecv[s, 0], 1, 1))

        def load(k):
            q = [state[s, c, k] for c in range(5)]
            prim = primitives(q)
            f, speed = normal_flux(q, prim, 0)
            return q, prim, f, speed

        def in_plane(k, q, prim):
            _, _, sound = prim
            speed = jnp.abs(prim[0][1]) + sound
            up, down = [], []
            for c in range(5):
                mirror = -q[c] if c == 2 else q[c]
                u = jnp.where(last_sub, rrecv[s, 1, c, k : k + 1, :], pltpu.roll(q[c], rows - 1, 0))
                d = jnp.where(first_sub, rrecv[s, 0, c, k : k + 1, :], pltpu.roll(q[c], 1, 0))
                up.append(jnp.where(wall_hi, mirror, u))
                down.append(jnp.where(wall_lo, mirror, d))
            fu, su = normal_flux(up, primitives(up), 1)
            fd, sd = normal_flux(down, primitives(down), 1)
            ju, jd = jump(speed, su, q, up), jump(sd, speed, down, q)
            acc = [(fu[c] - fd[c]) - (ju[c] - jd[c]) for c in range(5)]
            speed = jnp.abs(prim[0][2]) + sound
            after, before = [], []
            for c in range(5):
                place = c * ca + k
                edge = pltpu.roll(merged, cols - 1 - 2 * place, 1)
                after.append(jnp.where(last_lane, edge, pltpu.roll(q[c], cols - 1, 1)))
                before.append(jnp.where(first_lane, edge, pltpu.roll(q[c], 1, 1)))
            fa, sa = normal_flux(after, primitives(after), 2)
            fb, sb = normal_flux(before, primitives(before), 2)
            ja, jb = jump(speed, sa, q, after), jump(sb, speed, before, q)
            return [acc[c] + ((fa[c] - fb[c]) - (ja[c] - jb[c])) for c in range(5)]

        def finish(k, q, acc):
            new = []
            for c in range(5):
                advanced = q[c] + (-0.5 * COURANT) * acc[c]
                new.append(keep * state[base, c, k] + mix * advanced)
                state[s + 1, c, k] = new[c]
            return new

        q0, prim0, f0, s0 = load(0)
        here = load(1)
        j0 = jump(s0, here[3], q0, here[0])
        acc0 = in_plane(0, q0, prim0)
        acc0 = [acc0[c] + sigma * here[2][c] - j0[c] for c in range(5)]
        packed = zero
        toward_f, toward_j = f0, j0
        for k in range(1, ca):
            q, prim, f, speed = here
            if k + 1 < ca:
                here = load(k + 1)
            else:
                qf = [far[c] for c in range(5)]
                pf = primitives(qf)
                here = (qf, pf) + normal_flux(qf, pf, 0)
            j = jump(speed, here[3], q, here[0])
            acc = in_plane(k, q, prim)
            acc = [
                acc[c] + sigma * (here[2][c] - toward_f[c]) - (j[c] - toward_j[c]) for c in range(5)
            ]
            packed = pack(s + 1, k, finish(k, q, acc), packed)
            toward_f, toward_j = f, j

        offset = offsets_ref[step]
        cycle = nc * cols
        shift = jnp.where(is_rotor, offset, cycle - offset)
        start = lax.rem(me * cols + shift, cycle)
        block = lax.div(start, cols)
        turn = start - block * cols
        back = lax.rem(cols - turn, cols)
        following = lax.rem(block + 1, nc)
        for j in range(nc):
            gather_arrival(s, j).wait_recv()
        ghost = []
        want = jnp.where(lane >= turn, block, following)
        for c in range(5):
            both = grecv[s, 0, c]
            for j in range(1, nc):
                both = jnp.where(want == j, grecv[s, j, c], both)
            ghost.append(pltpu.roll(both, back, 1))
        swirl = ghost[3]
        ghost[4] = ghost[4] + sigma * swirl * blade + 0.5 * ghost[0] * blade * blade
        ghost[3] = swirl + sigma * ghost[0] * blade
        fg, sg = normal_flux(ghost, primitives(ghost), 0)
        jg = jump(sg, s0, ghost, q0)
        acc0 = [acc0[c] - sigma * fg[c] + jg[c] for c in range(5)]
        new = finish(0, q0, acc0)
        for c in range(5):
            gsend[s + 1, c] = new[c]

        @pl.when(s < total - 1)
        def _():
            start_gather(s + 1)

        csend[s + 1] = pack(s + 1, 0, new, packed)

        @pl.when(s < total - 1)
        def _():
            for copy in halo_copies(s + 1):
                copy.start()

        return carry

    lax.fori_loop(0, total, stage, 0)
    for k in range(ca):
        for c in range(5):
            out_ref[0, c, axial(k)] = state[total, c, k]

    def drain(s, carry):
        for d in range(nc):
            gather_copy(s, d).wait_send()
        for copy in halo_copies(s):
            copy.wait_send()
        return carry

    lax.fori_loop(0, total, drain, 0)


def solution(mesh):
    placed = (
        P("row", None, None, "rad", "circ"),
        P(None, "rad", "circ"),
        P(None, "rad", "circ"),
        P("rad"),
        P(),
    )
    nc, nr = mesh.shape["circ"], mesh.shape["rad"]

    def per_device(flow, inflow, outflow, wheel, offsets):
        _, comps, ca, rows, cols = flow.shape
        steps = offsets.shape[0]
        total = steps * STAGES
        vmem = pl.BlockSpec(memory_space=pltpu.VMEM)
        smem = pl.BlockSpec(memory_space=pltpu.SMEM)
        f32 = jnp.float32
        return pl.pallas_call(
            functools.partial(kernel, nc, nr, steps),
            out_shape=jax.ShapeDtypeStruct(flow.shape, f32),
            in_specs=[vmem, vmem, vmem, smem, smem],
            out_specs=vmem,
            scratch_shapes=[
                pltpu.VMEM((total + 1, comps, ca, rows, cols), f32),
                pltpu.VMEM((comps, rows, cols), f32),
                pltpu.VMEM((total + 1, comps, rows, cols), f32),
                pltpu.VMEM((total, nc, comps, rows, cols), f32),
                pltpu.VMEM((total + 1, rows, cols), f32),
                pltpu.VMEM((total, 2, rows, cols), f32),
                pltpu.VMEM((total + 1, 2, comps, ca, cols), f32),
                pltpu.VMEM((total, 2, comps, ca, cols), f32),
                pltpu.SemaphoreType.DMA((total, nc)),
                pltpu.SemaphoreType.DMA((total, nc)),
                pltpu.SemaphoreType.DMA((total, 4)),
                pltpu.SemaphoreType.DMA((total, 4)),
            ],
            compiler_params=pltpu.CompilerParams(
                collective_id=0, has_side_effects=True, vmem_limit_bytes=24 * 1024 * 1024),
        )(flow, inflow, outflow, wheel, offsets)

    return jax.shard_map(
        per_device,
        mesh=mesh,
        in_specs=placed,
        out_specs=P("row", None, None, "rad", "circ"),
        check_vma=False,
    )
```

```python
import functools

import jax
import jax.numpy as jnp
from jax import lax
from jax.experimental import pallas as pl
from jax.experimental.pallas import tpu as pltpu
from jax.sharding import PartitionSpec as P

GAMMA = 1.4
COURANT = 0.1
MESH = pl.DeviceIdType.MESH
STAGES = 3
CUT = 4


def layer_groups(ca):
    cut = min(1 + CUT, ca)
    return [g for g in ([0], list(range(1, cut)), list(range(cut, ca))) if g]


def primitives(q):
    inverse = 1.0 / q[0]
    vel = [q[1] * inverse, q[2] * inverse, q[3] * inverse]
    kinetic = 0.5 * (q[1] * vel[0] + q[2] * vel[1] + q[3] * vel[2])
    pressure = (GAMMA - 1.0) * (q[4] - kinetic)
    sound = jnp.sqrt(GAMMA * pressure * inverse)
    return vel, pressure, sound


def normal_flux(q, prim, k):
    vel, pressure, sound = prim
    v = vel[k]
    f = [q[1 + k], q[1] * v, q[2] * v, q[3] * v, (q[4] + pressure) * v]
    f[1 + k] = f[1 + k] + pressure
    return f, jnp.abs(v) + sound


def jump(speed_a, speed_b, left, right):
    s = jnp.maximum(speed_a, speed_b)
    return [s * (right[c] - left[c]) for c in range(5)]


def kernel(
    nc, nr, steps,
    flow_hbm, inflow_hbm, outflow_hbm, wheel_ref, offsets_ref,
    out_ref,
    flow_ref, ends, in_sem,
    state, far, gsend, grecv, csend, crecv, gs_sem, gr_sem, hs_sem, hr_sem, *rims,
):
    inputs = [
        pltpu.make_async_copy(src, dst, in_sem.at[i])
        for i, (src, dst) in enumerate(
            ((flow_hbm, flow_ref), (inflow_hbm, ends.at[0]), (outflow_hbm, ends.at[1])))
    ]
    for copy in inputs:
        copy.start()
    ca, rows, cols = state.shape[2:]
    total = steps * STAGES
    row = lax.axis_index("row")
    me = lax.axis_index("circ")
    rad = lax.axis_index("rad")
    is_rotor = row == 0
    groups = layer_groups(ca)
    rsends, rrecvs = rims[: len(groups)], rims[len(groups) :]
    other = 1 - row
    right, left = lax.rem(me + 1, nc), lax.rem(me + nc - 1, nc)
    above, below = lax.rem(rad + 1, nr), lax.rem(rad + nr - 1, nr)

    barrier = pltpu.get_barrier_semaphore()
    for d in range(nc):
        pl.semaphore_signal(
            barrier, inc=1, device_id=(other, lax.rem(me + d, nc), rad), device_id_type=MESH)
    for peer in ((row, right, rad), (row, left, rad), (row, me, above), (row, me, below)):
        pl.semaphore_signal(barrier, inc=1, device_id=peer, device_id_type=MESH)

    lane = lax.broadcasted_iota(jnp.int32, (rows, cols), 1)
    sub = lax.broadcasted_iota(jnp.int32, (rows, cols), 0)
    first_lane, last_lane = lane == 0, lane == cols - 1
    first_sub, last_sub = sub == 0, sub == rows - 1
    wall_lo = jnp.logical_and(first_sub, rad == 0)
    wall_hi = jnp.logical_and(last_sub, rad == nr - 1)
    pair = lax.div(lane, 2)
    even = lax.rem(lane, 2) == 0
    sigma = jnp.where(is_rotor, jnp.float32(-1.0), jnp.float32(1.0))
    blade = jnp.zeros((rows, cols), jnp.float32)
    for r in range(rows):
        blade = jnp.where(sub == r, wheel_ref[r], blade)

    def axial(k):
        return jnp.where(is_rotor, ca - 1 - k, k)

    def target(d):
        return jnp.where(2 * me < nc, nc - 1 - d, d)

    def gather_copy(slot, d):
        return pltpu.make_async_remote_copy(
            src_ref=gsend.at[slot], dst_ref=grecv.at[slot, me],
            send_sem=gs_sem.at[slot, d], recv_sem=gr_sem.at[slot, me],
            device_id=(other, target(d), rad), device_id_type=MESH)

    def gather_arrival(slot, j):
        return pltpu.make_async_remote_copy(
            src_ref=gsend.at[slot], dst_ref=grecv.at[slot, j],
            send_sem=gs_sem.at[slot, j], recv_sem=gr_sem.at[slot, j],
            device_id=(other, me, rad), device_id_type=MESH)

    def halo_copies(slot, g):
        plan = (
            (csend.at[slot, g], crecv.at[slot, g, 0], (row, right, rad)),
            (csend.at[slot, g], crecv.at[slot, g, 1], (row, left, rad)),
            (rsends[g].at[slot, 0], rrecvs[g].at[slot, 0], (row, me, above)),
            (rsends[g].at[slot, 1], rrecvs[g].at[slot, 1], (row, me, below)),
        )
        return [
            pltpu.make_async_remote_copy(
                src_ref=src, dst_ref=dst, send_sem=hs_sem.at[slot, g, i],
                recv_sem=hr_sem.at[slot, g, i], device_id=peer, device_id_type=MESH)
            for i, (src, dst, peer) in enumerate(plan)
        ]

    def start_halos(slot, g):
        for copy in halo_copies(slot, g):
            copy.start()

    def start_gather(slot):
        for d in range(nc):
            gather_copy(slot, d).start()

    def position(k, c):
        g = next(i for i, group in enumerate(groups) if k in group)
        return g, c * len(groups[g]) + groups[g].index(k)

    def pack(slot, k, q, packed):
        for c in range(5):
            g, place = position(k, c)
            rsends[g][slot, 0, place : place + 1, :] = q[c][rows - 1 : rows, :]
            rsends[g][slot, 1, place : place + 1, :] = q[c][0:1, :]
            packed = jnp.where(pair == place, pltpu.roll(q[c], 2 * place + 1, 1), packed)
        return packed

    zero = jnp.zeros((rows, cols), jnp.float32)
    for copy in inputs:
        copy.wait()
    for c in range(5):
        far[c] = jnp.where(is_rotor, ends[0, c], ends[1, c])
    for g, group in enumerate(groups):
        packed = zero
        for k in group:
            q = [flow_ref[0, c, axial(k)] for c in range(5)]
            for c in range(5):
                state[0, c, k] = q[c]
                if k == 0:
                    gsend[0, c] = q[c]
            packed = pack(0, k, q, packed)
        csend[0, g] = packed
    pl.semaphore_wait(barrier, nc + 4)
    start_gather(0)
    for g in list(range(1, len(groups))) + [0]:
        start_halos(0, g)

    def stage(s, carry):
        step = lax.div(s, STAGES)
        phase = s - step * STAGES
        base = step * STAGES
        keep = jnp.where(phase == 0, 0.0, jnp.where(phase == 1, 0.75, 1.0 / 3.0)).astype(jnp.float32)
        mix = jnp.where(phase == 0, 1.0, jnp.where(phase == 1, 0.25, 2.0 / 3.0)).astype(jnp.float32)

        def halos(g):
            for copy in halo_copies(s, g):
                copy.wait_recv()
            return jnp.where(
                even, pltpu.roll(crecv[s, g, 1], cols - 1, 1), pltpu.roll(crecv[s, g, 0], 1, 1))

        def send(g, packed):
            csend[s + 1, g] = packed

            @pl.when(s < total - 1)
            def _():
                start_halos(s + 1, g)

        def load(k):
            q = [state[s, c, k] for c in range(5)]
            prim = primitives(q)
            f, speed = normal_flux(q, prim, 0)
            return q, prim, f, speed

        def in_plane(k, q, prim, merged):
            _, _, sound = prim
            speed = jnp.abs(prim[0][1]) + sound
            up, down = [], []
            for c in range(5):
                mirror = -q[c] if c == 2 else q[c]
                g, place = position(k, c)
                rim = rrecvs[g]
                u = jnp.where(last_sub, rim[s, 1, place : place + 1, :], pltpu.roll(q[c], rows - 1, 0))
                d = jnp.where(first_sub, rim[s, 0, place : place + 1, :], pltpu.roll(q[c], 1, 0))
                up.append(jnp.where(wall_hi, mirror, u))
                down.append(jnp.where(wall_lo, mirror, d))
            fu, su = normal_flux(up, primitives(up), 1)
            fd, sd = normal_flux(down, primitives(down), 1)
            ju, jd = jump(speed, su, q, up), jump(sd, speed, down, q)
            acc = [(fu[c] - fd[c]) - (ju[c] - jd[c]) for c in range(5)]
            speed = jnp.abs(prim[0][2]) + sound
            after, before = [], []
            for c in range(5):
                _, place = position(k, c)
                edge = pltpu.roll(merged, cols - 1 - 2 * place, 1)
                after.append(jnp.where(last_lane, edge, pltpu.roll(q[c], cols - 1, 1)))
                before.append(jnp.where(first_lane, edge, pltpu.roll(q[c], 1, 1)))
            fa, sa = normal_flux(after, primitives(after), 2)
            fb, sb = normal_flux(before, primitives(before), 2)
            ja, jb = jump(speed, sa, q, after), jump(sb, speed, before, q)
            return [acc[c] + ((fa[c] - fb[c]) - (ja[c] - jb[c])) for c in range(5)]

        def finish(k, q, acc):
            new = []
            for c in range(5):
                advanced = q[c] + (-0.5 * COURANT) * acc[c]
                new.append(keep * state[base, c, k] + mix * advanced)
                state[s + 1, c, k] = new[c]
            return new

        q0, prim0, f0, s0 = load(0)
        here = load(1)
        j0 = jump(s0, here[3], q0, here[0])
        axial0 = [sigma * here[2][c] - j0[c] for c in range(5)]
        toward_f, toward_j = f0, j0
        for g in range(1, len(groups)):
            merged = halos(g)
            packed = zero
            for k in groups[g]:
                q, prim, f, speed = here
                if k + 1 < ca:
                    here = load(k + 1)
                else:
                    qf = [far[c] for c in range(5)]
                    pf = primitives(qf)
                    here = (qf, pf) + normal_flux(qf, pf, 0)
                j = jump(speed, here[3], q, here[0])
                acc = in_plane(k, q, prim, merged)
                acc = [
                    acc[c] + sigma * (here[2][c] - toward_f[c]) - (j[c] - toward_j[c])
                    for c in range(5)
                ]
                packed = pack(s + 1, k, finish(k, q, acc), packed)
                toward_f, toward_j = f, j
            send(g, packed)
        acc0 = in_plane(0, q0, prim0, halos(0))
        acc0 = [acc0[c] + axial0[c] for c in range(5)]

        offset = offsets_ref[step]
        cycle = nc * cols
        shift = jnp.where(is_rotor, offset, cycle - offset)
        start = lax.rem(me * cols + shift, cycle)
        block = lax.div(start, cols)
        turn = start - block * cols
        back = lax.rem(cols - turn, cols)
        following = lax.rem(block + 1, nc)
        for j in range(nc):
            gather_arrival(s, j).wait_recv()
        ghost = []
        want = jnp.where(lane >= turn, block, following)
        for c in range(5):
            both = grecv[s, 0, c]
            for j in range(1, nc):
                both = jnp.where(want == j, grecv[s, j, c], both)
            ghost.append(pltpu.roll(both, back, 1))
        swirl = ghost[3]
        ghost[4] = ghost[4] + sigma * swirl * blade + 0.5 * ghost[0] * blade * blade
        ghost[3] = swirl + sigma * ghost[0] * blade
        fg, sg = normal_flux(ghost, primitives(ghost), 0)
        jg = jump(sg, s0, ghost, q0)
        acc0 = [acc0[c] - sigma * fg[c] + jg[c] for c in range(5)]
        new = finish(0, q0, acc0)
        for c in range(5):
            gsend[s + 1, c] = new[c]

        @pl.when(s < total - 1)
        def _():
            start_gather(s + 1)

        send(0, pack(s + 1, 0, new, zero))
        return carry

    lax.fori_loop(0, total, stage, 0)
    for k in range(ca):
        for c in range(5):
            out_ref[0, c, axial(k)] = state[total, c, k]

    def drain(s, carry):
        for d in range(nc):
            gather_copy(s, d).wait_send()
        for g in range(len(groups)):
            for copy in halo_copies(s, g):
                copy.wait_send()
        return carry

    lax.fori_loop(0, total, drain, 0)


def solution(mesh):
    placed = (
        P("row", None, None, "rad", "circ"),
        P(None, "rad", "circ"),
        P(None, "rad", "circ"),
        P("rad"),
        P(),
    )
    nc, nr = mesh.shape["circ"], mesh.shape["rad"]

    def per_device(flow, inflow, outflow, wheel, offsets):
        _, comps, ca, rows, cols = flow.shape
        steps = offsets.shape[0]
        total = steps * STAGES
        vmem = pl.BlockSpec(memory_space=pltpu.VMEM)
        smem = pl.BlockSpec(memory_space=pltpu.SMEM)
        hbm = pl.BlockSpec(memory_space=pltpu.HBM)
        f32 = jnp.float32
        groups = layer_groups(ca)
        rims = [-(-comps * len(group) // 8) * 8 for group in groups]
        return pl.pallas_call(
            functools.partial(kernel, nc, nr, steps),
            out_shape=jax.ShapeDtypeStruct(flow.shape, f32),
            in_specs=[hbm, hbm, hbm, smem, smem],
            out_specs=vmem,
            scratch_shapes=[
                pltpu.VMEM(flow.shape, f32),
                pltpu.VMEM((2, comps, rows, cols), f32),
                pltpu.SemaphoreType.DMA((3,)),
                pltpu.VMEM((total + 1, comps, ca, rows, cols), f32),
                pltpu.VMEM((comps, rows, cols), f32),
                pltpu.VMEM((total + 1, comps, rows, cols), f32),
                pltpu.VMEM((total, nc, comps, rows, cols), f32),
                pltpu.VMEM((total + 1, len(groups), rows, cols), f32),
                pltpu.VMEM((total, len(groups), 2, rows, cols), f32),
                pltpu.SemaphoreType.DMA((total, nc)),
                pltpu.SemaphoreType.DMA((total, nc)),
                pltpu.SemaphoreType.DMA((total, len(groups), 4)),
                pltpu.SemaphoreType.DMA((total, len(groups), 4)),
                *[pltpu.VMEM((total + 1, 2, rim, cols), f32) for rim in rims],
                *[pltpu.VMEM((total, 2, rim, cols), f32) for rim in rims],
            ],
            compiler_params=pltpu.CompilerParams(
                collective_id=0, has_side_effects=True, vmem_limit_bytes=24 * 1024 * 1024),
        )(flow, inflow, outflow, wheel, offsets)

    return jax.shard_map(
        per_device,
        mesh=mesh,
        in_specs=placed,
        out_specs=P("row", None, None, "rad", "circ"),
        check_vma=False,
    )
```

```python
import functools

import jax
import jax.numpy as jnp
from jax import lax
from jax.experimental import pallas as pl
from jax.experimental.pallas import tpu as pltpu
from jax.sharding import PartitionSpec as P

GAMMA = 1.4
COURANT = 0.1
MESH = pl.DeviceIdType.MESH
STAGES = 3
CUT = 7


def layer_groups(ca):
    cut = min(1 + CUT, ca)
    return [g for g in ([0], list(range(1, cut)), list(range(cut, ca))) if g]


def primitives(q):
    inverse = 1.0 / q[0]
    vel = [q[1] * inverse, q[2] * inverse, q[3] * inverse]
    kinetic = 0.5 * (q[1] * vel[0] + q[2] * vel[1] + q[3] * vel[2])
    pressure = (GAMMA - 1.0) * (q[4] - kinetic)
    sound = jnp.sqrt(GAMMA * pressure * inverse)
    return vel, pressure, sound


def normal_flux(q, prim, k):
    vel, pressure, sound = prim
    v = vel[k]
    f = [q[1 + k], q[1] * v, q[2] * v, q[3] * v, (q[4] + pressure) * v]
    f[1 + k] = f[1 + k] + pressure
    return f, jnp.abs(v) + sound


def jump(speed_a, speed_b, left, right):
    s = jnp.maximum(speed_a, speed_b)
    return [s * (right[c] - left[c]) for c in range(5)]


def kernel(
    nc, nr, steps,
    flow_hbm, inflow_hbm, outflow_hbm, wheel_ref, offsets_ref,
    out_ref,
    flow_ref, ends, in_sem,
    state, far, gsend, grecv, csend, crecv, gs_sem, gr_sem, hs_sem, hr_sem, *rims,
):
    inputs = [
        pltpu.make_async_copy(src, dst, in_sem.at[i])
        for i, (src, dst) in enumerate(
            ((flow_hbm, flow_ref), (inflow_hbm, ends.at[0]), (outflow_hbm, ends.at[1])))
    ]
    for copy in inputs:
        copy.start()
    ca, rows, cols = state.shape[2:]
    total = steps * STAGES
    row = lax.axis_index("row")
    me = lax.axis_index("circ")
    rad = lax.axis_index("rad")
    is_rotor = row == 0
    groups = layer_groups(ca)
    rsends, rrecvs = rims[: len(groups)], rims[len(groups) :]
    other = 1 - row
    right, left = lax.rem(me + 1, nc), lax.rem(me + nc - 1, nc)
    above, below = lax.rem(rad + 1, nr), lax.rem(rad + nr - 1, nr)

    barrier = pltpu.get_barrier_semaphore()
    for d in range(nc):
        pl.semaphore_signal(
            barrier, inc=1, device_id=(other, lax.rem(me + d, nc), rad), device_id_type=MESH)
    for peer in ((row, right, rad), (row, left, rad), (row, me, above), (row, me, below)):
        pl.semaphore_signal(barrier, inc=1, device_id=peer, device_id_type=MESH)

    lane = lax.broadcasted_iota(jnp.int32, (rows, cols), 1)
    sub = lax.broadcasted_iota(jnp.int32, (rows, cols), 0)
    first_lane, last_lane = lane == 0, lane == cols - 1
    first_sub, last_sub = sub == 0, sub == rows - 1
    wall_lo = jnp.logical_and(first_sub, rad == 0)
    wall_hi = jnp.logical_and(last_sub, rad == nr - 1)
    pair = lax.div(lane, 2)
    even = lax.rem(lane, 2) == 0
    sigma = jnp.where(is_rotor, jnp.float32(-1.0), jnp.float32(1.0))
    blade = jnp.zeros((rows, cols), jnp.float32)
    for r in range(rows):
        blade = jnp.where(sub == r, wheel_ref[r], blade)

    def axial(k):
        return jnp.where(is_rotor, ca - 1 - k, k)

    def target(d):
        return jnp.where(2 * me < nc, nc - 1 - d, d)

    def gather_copy(slot, d):
        return pltpu.make_async_remote_copy(
            src_ref=gsend.at[slot], dst_ref=grecv.at[slot, me],
            send_sem=gs_sem.at[slot, d], recv_sem=gr_sem.at[slot, me],
            device_id=(other, target(d), rad), device_id_type=MESH)

    def gather_arrival(slot, j):
        return pltpu.make_async_remote_copy(
            src_ref=gsend.at[slot], dst_ref=grecv.at[slot, j],
            send_sem=gs_sem.at[slot, j], recv_sem=gr_sem.at[slot, j],
            device_id=(other, me, rad), device_id_type=MESH)

    def halo_copies(slot, g):
        plan = (
            (csend.at[slot, g], crecv.at[slot, g, 0], (row, right, rad)),
            (csend.at[slot, g], crecv.at[slot, g, 1], (row, left, rad)),
            (rsends[g].at[slot, 0], rrecvs[g].at[slot, 0], (row, me, above)),
            (rsends[g].at[slot, 1], rrecvs[g].at[slot, 1], (row, me, below)),
        )
        return [
            pltpu.make_async_remote_copy(
                src_ref=src, dst_ref=dst, send_sem=hs_sem.at[slot, g, i],
                recv_sem=hr_sem.at[slot, g, i], device_id=peer, device_id_type=MESH)
            for i, (src, dst, peer) in enumerate(plan)
        ]

    def start_halos(slot, g):
        for copy in halo_copies(slot, g):
            copy.start()

    def start_gather(slot):
        for d in range(nc):
            gather_copy(slot, d).start()

    def position(k, c):
        g = next(i for i, group in enumerate(groups) if k in group)
        return g, c * len(groups[g]) + groups[g].index(k)

    def pack(slot, k, q, packed):
        for c in range(5):
            g, place = position(k, c)
            rsends[g][slot, 0, place : place + 1, :] = q[c][rows - 1 : rows, :]
            rsends[g][slot, 1, place : place + 1, :] = q[c][0:1, :]
            packed = jnp.where(pair == place, pltpu.roll(q[c], 2 * place + 1, 1), packed)
        return packed

    zero = jnp.zeros((rows, cols), jnp.float32)
    for copy in inputs:
        copy.wait()
    for c in range(5):
        far[c] = jnp.where(is_rotor, ends[0, c], ends[1, c])
    for g, group in enumerate(groups):
        packed = zero
        for k in group:
            q = [flow_ref[0, c, axial(k)] for c in range(5)]
            for c in range(5):
                state[0, c, k] = q[c]
                if k == 0:
                    gsend[0, c] = q[c]
            packed = pack(0, k, q, packed)
        csend[0, g] = packed
    pl.semaphore_wait(barrier, nc + 4)
    start_gather(0)
    for g in list(range(1, len(groups))) + [0]:
        start_halos(0, g)

    def stage(s, carry):
        step = lax.div(s, STAGES)
        phase = s - step * STAGES
        base = step * STAGES
        keep = jnp.where(phase == 0, 0.0, jnp.where(phase == 1, 0.75, 1.0 / 3.0)).astype(jnp.float32)
        mix = jnp.where(phase == 0, 1.0, jnp.where(phase == 1, 0.25, 2.0 / 3.0)).astype(jnp.float32)

        def halos(g):
            for copy in halo_copies(s, g):
                copy.wait_recv()
            return jnp.where(
                even, pltpu.roll(crecv[s, g, 1], cols - 1, 1), pltpu.roll(crecv[s, g, 0], 1, 1))

        def send(g, packed):
            csend[s + 1, g] = packed

            @pl.when(s < total - 1)
            def _():
                start_halos(s + 1, g)

        def load(k):
            q = [state[s, c, k] for c in range(5)]
            prim = primitives(q)
            f, speed = normal_flux(q, prim, 0)
            return q, prim, f, speed

        def in_plane(k, q, prim, merged):
            _, _, sound = prim
            speed = jnp.abs(prim[0][1]) + sound
            up, down = [], []
            for c in range(5):
                mirror = -q[c] if c == 2 else q[c]
                g, place = position(k, c)
                rim = rrecvs[g]
                u = jnp.where(last_sub, rim[s, 1, place : place + 1, :], pltpu.roll(q[c], rows - 1, 0))
                d = jnp.where(first_sub, rim[s, 0, place : place + 1, :], pltpu.roll(q[c], 1, 0))
                up.append(jnp.where(wall_hi, mirror, u))
                down.append(jnp.where(wall_lo, mirror, d))
            fu, su = normal_flux(up, primitives(up), 1)
            fd, sd = normal_flux(down, primitives(down), 1)
            ju, jd = jump(speed, su, q, up), jump(sd, speed, down, q)
            acc = [(fu[c] - fd[c]) - (ju[c] - jd[c]) for c in range(5)]
            speed = jnp.abs(prim[0][2]) + sound
            after, before = [], []
            for c in range(5):
                _, place = position(k, c)
                edge = pltpu.roll(merged, cols - 1 - 2 * place, 1)
                after.append(jnp.where(last_lane, edge, pltpu.roll(q[c], cols - 1, 1)))
                before.append(jnp.where(first_lane, edge, pltpu.roll(q[c], 1, 1)))
            fa, sa = normal_flux(after, primitives(after), 2)
            fb, sb = normal_flux(before, primitives(before), 2)
            ja, jb = jump(speed, sa, q, after), jump(sb, speed, before, q)
            return [acc[c] + ((fa[c] - fb[c]) - (ja[c] - jb[c])) for c in range(5)]

        def finish(k, q, acc):
            new = []
            for c in range(5):
                advanced = q[c] + (-0.5 * COURANT) * acc[c]
                new.append(keep * state[base, c, k] + mix * advanced)
                state[s + 1, c, k] = new[c]
            return new

        q0, prim0, f0, s0 = load(0)
        here = load(1)
        j0 = jump(s0, here[3], q0, here[0])
        axial0 = [sigma * here[2][c] - j0[c] for c in range(5)]
        toward_f, toward_j = f0, j0
        for g in range(1, len(groups)):
            merged = halos(g)
            packed = zero
            for k in groups[g]:
                q, prim, f, speed = here
                if k + 1 < ca:
                    here = load(k + 1)
                else:
                    qf = [far[c] for c in range(5)]
                    pf = primitives(qf)
                    here = (qf, pf) + normal_flux(qf, pf, 0)
                j = jump(speed, here[3], q, here[0])
                acc = in_plane(k, q, prim, merged)
                acc = [
                    acc[c] + sigma * (here[2][c] - toward_f[c]) - (j[c] - toward_j[c])
                    for c in range(5)
                ]
                packed = pack(s + 1, k, finish(k, q, acc), packed)
                toward_f, toward_j = f, j
            send(g, packed)
        acc0 = in_plane(0, q0, prim0, halos(0))
        acc0 = [acc0[c] + axial0[c] for c in range(5)]

        offset = offsets_ref[step]
        cycle = nc * cols
        shift = jnp.where(is_rotor, offset, cycle - offset)
        start = lax.rem(me * cols + shift, cycle)
        block = lax.div(start, cols)
        turn = start - block * cols
        back = lax.rem(cols - turn, cols)
        following = lax.rem(block + 1, nc)
        for j in range(nc):
            gather_arrival(s, j).wait_recv()
        ghost = []
        want = jnp.where(lane >= turn, block, following)
        for c in range(5):
            both = grecv[s, 0, c]
            for j in range(1, nc):
                both = jnp.where(want == j, grecv[s, j, c], both)
            ghost.append(pltpu.roll(both, back, 1))
        swirl = ghost[3]
        ghost[4] = ghost[4] + sigma * swirl * blade + 0.5 * ghost[0] * blade * blade
        ghost[3] = swirl + sigma * ghost[0] * blade
        fg, sg = normal_flux(ghost, primitives(ghost), 0)
        jg = jump(sg, s0, ghost, q0)
        acc0 = [acc0[c] - sigma * fg[c] + jg[c] for c in range(5)]
        new = finish(0, q0, acc0)
        for c in range(5):
            gsend[s + 1, c] = new[c]

        csend[s + 1, 0] = pack(s + 1, 0, new, zero)

        @pl.when(s < total - 1)
        def _():
            copies = halo_copies(s + 1, 0)
            for copy in copies[:2]:
                copy.start()
            start_gather(s + 1)
            for copy in copies[2:]:
                copy.start()

        return carry

    lax.fori_loop(0, total, stage, 0)
    for k in range(ca):
        for c in range(5):
            out_ref[0, c, axial(k)] = state[total, c, k]

    def drain(s, carry):
        for d in range(nc):
            gather_copy(s, d).wait_send()
        for g in range(len(groups)):
            for copy in halo_copies(s, g):
                copy.wait_send()
        return carry

    lax.fori_loop(0, total, drain, 0)


def solution(mesh):
    placed = (
        P("row", None, None, "rad", "circ"),
        P(None, "rad", "circ"),
        P(None, "rad", "circ"),
        P("rad"),
        P(),
    )
    nc, nr = mesh.shape["circ"], mesh.shape["rad"]

    def per_device(flow, inflow, outflow, wheel, offsets):
        _, comps, ca, rows, cols = flow.shape
        steps = offsets.shape[0]
        total = steps * STAGES
        vmem = pl.BlockSpec(memory_space=pltpu.VMEM)
        smem = pl.BlockSpec(memory_space=pltpu.SMEM)
        hbm = pl.BlockSpec(memory_space=pltpu.HBM)
        f32 = jnp.float32
        groups = layer_groups(ca)
        rims = [-(-comps * len(group) // 8) * 8 for group in groups]
        return pl.pallas_call(
            functools.partial(kernel, nc, nr, steps),
            out_shape=jax.ShapeDtypeStruct(flow.shape, f32),
            in_specs=[hbm, hbm, hbm, smem, smem],
            out_specs=vmem,
            scratch_shapes=[
                pltpu.VMEM(flow.shape, f32),
                pltpu.VMEM((2, comps, rows, cols), f32),
                pltpu.SemaphoreType.DMA((3,)),
                pltpu.VMEM((total + 1, comps, ca, rows, cols), f32),
                pltpu.VMEM((comps, rows, cols), f32),
                pltpu.VMEM((total + 1, comps, rows, cols), f32),
                pltpu.VMEM((total, nc, comps, rows, cols), f32),
                pltpu.VMEM((total + 1, len(groups), rows, cols), f32),
                pltpu.VMEM((total, len(groups), 2, rows, cols), f32),
                pltpu.SemaphoreType.DMA((total, nc)),
                pltpu.SemaphoreType.DMA((total, nc)),
                pltpu.SemaphoreType.DMA((total, len(groups), 4)),
                pltpu.SemaphoreType.DMA((total, len(groups), 4)),
                *[pltpu.VMEM((total + 1, 2, rim, cols), f32) for rim in rims],
                *[pltpu.VMEM((total, 2, rim, cols), f32) for rim in rims],
            ],
            compiler_params=pltpu.CompilerParams(
                collective_id=0, has_side_effects=True, vmem_limit_bytes=60 * 1024 * 1024),
        )(flow, inflow, outflow, wheel, offsets)

    return jax.shard_map(
        per_device,
        mesh=mesh,
        in_specs=placed,
        out_specs=P("row", None, None, "rad", "circ"),
        check_vma=False,
    )
```

```python
import functools

import jax
import jax.numpy as jnp
from jax import lax
from jax.experimental import pallas as pl
from jax.experimental.pallas import tpu as pltpu
from jax.sharding import PartitionSpec as P

GAMMA = 1.4
COURANT = 0.1
MESH = pl.DeviceIdType.MESH
STAGES = 3
CUT = 4


def layer_groups(ca):
    cut = min(1 + CUT, ca)
    return [g for g in ([0], list(range(1, cut)), list(range(cut, ca))) if g]


def primitives(q):
    inverse = 1.0 / q[0]
    vel = [q[1] * inverse, q[2] * inverse, q[3] * inverse]
    kinetic = 0.5 * (q[1] * vel[0] + q[2] * vel[1] + q[3] * vel[2])
    pressure = (GAMMA - 1.0) * (q[4] - kinetic)
    sound = jnp.sqrt(GAMMA * pressure * inverse)
    return vel, pressure, sound


def normal_flux(q, prim, k):
    vel, pressure, sound = prim
    v = vel[k]
    f = [q[1 + k], q[1] * v, q[2] * v, q[3] * v, (q[4] + pressure) * v]
    f[1 + k] = f[1 + k] + pressure
    return f, jnp.abs(v) + sound


def jump(speed_a, speed_b, left, right):
    s = jnp.maximum(speed_a, speed_b)
    return [s * (right[c] - left[c]) for c in range(5)]


def kernel(
    nc, nr, steps,
    flow_hbm, inflow_hbm, outflow_hbm, wheel_ref, offsets_ref,
    out_ref,
    flow_ref, ends, in_sem,
    state, far, gsend, grecv, csend, crecv, gs_sem, gr_sem, hs_sem, hr_sem, *rims,
):
    inputs = [
        pltpu.make_async_copy(src, dst, in_sem.at[i])
        for i, (src, dst) in enumerate(
            ((flow_hbm, flow_ref), (inflow_hbm, ends.at[0]), (outflow_hbm, ends.at[1])))
    ]
    for copy in inputs:
        copy.start()
    ca, rows, cols = state.shape[2:]
    total = steps * STAGES
    row = lax.axis_index("row")
    me = lax.axis_index("circ")
    rad = lax.axis_index("rad")
    is_rotor = row == 0
    groups = layer_groups(ca)
    rsends, rrecvs = rims[: len(groups)], rims[len(groups) :]
    other = 1 - row
    right, left = lax.rem(me + 1, nc), lax.rem(me + nc - 1, nc)
    above, below = lax.rem(rad + 1, nr), lax.rem(rad + nr - 1, nr)

    barrier = pltpu.get_barrier_semaphore()
    for d in range(nc):
        pl.semaphore_signal(
            barrier, inc=1, device_id=(other, lax.rem(me + d, nc), rad), device_id_type=MESH)
    for peer in ((row, right, rad), (row, left, rad), (row, me, above), (row, me, below)):
        pl.semaphore_signal(barrier, inc=1, device_id=peer, device_id_type=MESH)

    lane = lax.broadcasted_iota(jnp.int32, (rows, cols), 1)
    sub = lax.broadcasted_iota(jnp.int32, (rows, cols), 0)
    first_lane, last_lane = lane == 0, lane == cols - 1
    first_sub, last_sub = sub == 0, sub == rows - 1
    wall_lo = jnp.logical_and(first_sub, rad == 0)
    wall_hi = jnp.logical_and(last_sub, rad == nr - 1)
    pair = lax.div(lane, 2)
    even = lax.rem(lane, 2) == 0
    sigma = jnp.where(is_rotor, jnp.float32(-1.0), jnp.float32(1.0))
    blade = jnp.zeros((rows, cols), jnp.float32)
    for r in range(rows):
        blade = jnp.where(sub == r, wheel_ref[r], blade)

    def axial(k):
        return jnp.where(is_rotor, ca - 1 - k, k)

    def target(d):
        return jnp.where(2 * me < nc, nc - 1 - d, d)

    def gather_copy(slot, d):
        return pltpu.make_async_remote_copy(
            src_ref=gsend.at[slot], dst_ref=grecv.at[slot, me],
            send_sem=gs_sem.at[slot, d], recv_sem=gr_sem.at[slot, me],
            device_id=(other, target(d), rad), device_id_type=MESH)

    def gather_arrival(slot, j):
        return pltpu.make_async_remote_copy(
            src_ref=gsend.at[slot], dst_ref=grecv.at[slot, j],
            send_sem=gs_sem.at[slot, j], recv_sem=gr_sem.at[slot, j],
            device_id=(other, me, rad), device_id_type=MESH)

    def halo_copies(slot, g):
        plan = (
            (csend.at[slot, g], crecv.at[slot, g, 0], (row, right, rad)),
            (csend.at[slot, g], crecv.at[slot, g, 1], (row, left, rad)),
            (rsends[g].at[slot, 0], rrecvs[g].at[slot, 0], (row, me, above)),
            (rsends[g].at[slot, 1], rrecvs[g].at[slot, 1], (row, me, below)),
        )
        return [
            pltpu.make_async_remote_copy(
                src_ref=src, dst_ref=dst, send_sem=hs_sem.at[slot, g, i],
                recv_sem=hr_sem.at[slot, g, i], device_id=peer, device_id_type=MESH)
            for i, (src, dst, peer) in enumerate(plan)
        ]

    def start_halos(slot, g):
        for copy in halo_copies(slot, g):
            copy.start()

    def start_gather(slot):
        for d in range(nc):
            gather_copy(slot, d).start()

    def position(k, c):
        g = next(i for i, group in enumerate(groups) if k in group)
        return g, c * len(groups[g]) + groups[g].index(k)

    def pack(slot, k, q, packed):
        for c in range(5):
            g, place = position(k, c)
            rsends[g][slot, 0, place : place + 1, :] = q[c][rows - 1 : rows, :]
            rsends[g][slot, 1, place : place + 1, :] = q[c][0:1, :]
            packed = jnp.where(pair == place, pltpu.roll(q[c], 2 * place + 1, 1), packed)
        return packed

    zero = jnp.zeros((rows, cols), jnp.float32)
    for copy in inputs:
        copy.wait()
    for c in range(5):
        far[c] = jnp.where(is_rotor, ends[0, c], ends[1, c])
    for g, group in enumerate(groups):
        packed = zero
        for k in group:
            q = [flow_ref[0, c, axial(k)] for c in range(5)]
            for c in range(5):
                state[0, c, k] = q[c]
                if k == 0:
                    gsend[0, c] = q[c]
            packed = pack(0, k, q, packed)
        csend[0, g] = packed
    pl.semaphore_wait(barrier, nc + 4)
    start_gather(0)
    for g in list(range(1, len(groups))) + [0]:
        start_halos(0, g)

    def stage(s, carry):
        step = lax.div(s, STAGES)
        phase = s - step * STAGES
        base = step * STAGES
        keep = jnp.where(phase == 0, 0.0, jnp.where(phase == 1, 0.75, 1.0 / 3.0)).astype(jnp.float32)
        mix = jnp.where(phase == 0, 1.0, jnp.where(phase == 1, 0.25, 2.0 / 3.0)).astype(jnp.float32)

        def halos(g):
            for copy in halo_copies(s, g):
                copy.wait_recv()
            return jnp.where(
                even, pltpu.roll(crecv[s, g, 1], cols - 1, 1), pltpu.roll(crecv[s, g, 0], 1, 1))

        def send(g, packed):
            csend[s + 1, g] = packed

            @pl.when(s < total - 1)
            def _():
                start_halos(s + 1, g)

        def load(k):
            q = [state[s, c, k] for c in range(5)]
            prim = primitives(q)
            f, speed = normal_flux(q, prim, 0)
            return q, prim, f, speed

        def in_plane(k, q, prim, merged):
            _, _, sound = prim
            speed = jnp.abs(prim[0][1]) + sound
            up, down = [], []
            for c in range(5):
                mirror = -q[c] if c == 2 else q[c]
                g, place = position(k, c)
                rim = rrecvs[g]
                u = jnp.where(last_sub, rim[s, 1, place : place + 1, :], pltpu.roll(q[c], rows - 1, 0))
                d = jnp.where(first_sub, rim[s, 0, place : place + 1, :], pltpu.roll(q[c], 1, 0))
                up.append(jnp.where(wall_hi, mirror, u))
                down.append(jnp.where(wall_lo, mirror, d))
            fu, su = normal_flux(up, primitives(up), 1)
            fd, sd = normal_flux(down, primitives(down), 1)
            ju, jd = jump(speed, su, q, up), jump(sd, speed, down, q)
            acc = [(fu[c] - fd[c]) - (ju[c] - jd[c]) for c in range(5)]
            speed = jnp.abs(prim[0][2]) + sound
            after, before = [], []
            for c in range(5):
                _, place = position(k, c)
                edge = pltpu.roll(merged, cols - 1 - 2 * place, 1)
                after.append(jnp.where(last_lane, edge, pltpu.roll(q[c], cols - 1, 1)))
                before.append(jnp.where(first_lane, edge, pltpu.roll(q[c], 1, 1)))
            fa, sa = normal_flux(after, primitives(after), 2)
            fb, sb = normal_flux(before, primitives(before), 2)
            ja, jb = jump(speed, sa, q, after), jump(sb, speed, before, q)
            return [acc[c] + ((fa[c] - fb[c]) - (ja[c] - jb[c])) for c in range(5)]

        def finish(k, q, acc):
            new = []
            for c in range(5):
                advanced = q[c] + (-0.5 * COURANT) * acc[c]
                new.append(keep * state[base, c, k] + mix * advanced)
                state[s + 1, c, k] = new[c]
            return new

        q0, prim0, f0, s0 = load(0)
        here = load(1)
        j0 = jump(s0, here[3], q0, here[0])
        axial0 = [sigma * here[2][c] - j0[c] for c in range(5)]
        toward_f, toward_j = f0, j0
        for g in range(1, len(groups)):
            merged = halos(g)
            packed = zero
            for k in groups[g]:
                q, prim, f, speed = here
                if k + 1 < ca:
                    here = load(k + 1)
                else:
                    qf = [far[c] for c in range(5)]
                    pf = primitives(qf)
                    here = (qf, pf) + normal_flux(qf, pf, 0)
                j = jump(speed, here[3], q, here[0])
                acc = in_plane(k, q, prim, merged)
                acc = [
                    acc[c] + sigma * (here[2][c] - toward_f[c]) - (j[c] - toward_j[c])
                    for c in range(5)
                ]
                packed = pack(s + 1, k, finish(k, q, acc), packed)
                toward_f, toward_j = f, j
            send(g, packed)
        acc0 = in_plane(0, q0, prim0, halos(0))
        acc0 = [acc0[c] + axial0[c] for c in range(5)]

        offset = offsets_ref[step]
        cycle = nc * cols
        shift = jnp.where(is_rotor, offset, cycle - offset)
        start = lax.rem(me * cols + shift, cycle)
        block = lax.div(start, cols)
        turn = start - block * cols
        back = lax.rem(cols - turn, cols)
        following = lax.rem(block + 1, nc)
        for j in range(nc):
            gather_arrival(s, j).wait_recv()
        ghost = []
        want = jnp.where(lane >= turn, block, following)
        for c in range(5):
            both = grecv[s, 0, c]
            for j in range(1, nc):
                both = jnp.where(want == j, grecv[s, j, c], both)
            ghost.append(pltpu.roll(both, back, 1))
        swirl = ghost[3]
        ghost[4] = ghost[4] + sigma * swirl * blade + 0.5 * ghost[0] * blade * blade
        ghost[3] = swirl + sigma * ghost[0] * blade
        fg, sg = normal_flux(ghost, primitives(ghost), 0)
        jg = jump(sg, s0, ghost, q0)
        acc0 = [acc0[c] - sigma * fg[c] + jg[c] for c in range(5)]
        new = finish(0, q0, acc0)
        for c in range(5):
            gsend[s + 1, c] = new[c]

        csend[s + 1, 0] = pack(s + 1, 0, new, zero)

        @pl.when(s < total - 1)
        def _():
            copies = halo_copies(s + 1, 0)
            for copy in copies:
                copy.start()
            start_gather(s + 1)

        return carry

    lax.fori_loop(0, total, stage, 0)
    for k in range(ca):
        for c in range(5):
            out_ref[0, c, axial(k)] = state[total, c, k]

    def drain(s, carry):
        for d in range(nc):
            gather_copy(s, d).wait_send()
        for g in range(len(groups)):
            for copy in halo_copies(s, g):
                copy.wait_send()
        return carry

    lax.fori_loop(0, total, drain, 0)


def solution(mesh):
    placed = (
        P("row", None, None, "rad", "circ"),
        P(None, "rad", "circ"),
        P(None, "rad", "circ"),
        P("rad"),
        P(),
    )
    nc, nr = mesh.shape["circ"], mesh.shape["rad"]

    def per_device(flow, inflow, outflow, wheel, offsets):
        _, comps, ca, rows, cols = flow.shape
        steps = offsets.shape[0]
        total = steps * STAGES
        vmem = pl.BlockSpec(memory_space=pltpu.VMEM)
        smem = pl.BlockSpec(memory_space=pltpu.SMEM)
        hbm = pl.BlockSpec(memory_space=pltpu.HBM)
        f32 = jnp.float32
        groups = layer_groups(ca)
        rims = [-(-comps * len(group) // 8) * 8 for group in groups]
        return pl.pallas_call(
            functools.partial(kernel, nc, nr, steps),
            out_shape=jax.ShapeDtypeStruct(flow.shape, f32),
            in_specs=[hbm, hbm, hbm, smem, smem],
            out_specs=vmem,
            scratch_shapes=[
                pltpu.VMEM(flow.shape, f32),
                pltpu.VMEM((2, comps, rows, cols), f32),
                pltpu.SemaphoreType.DMA((3,)),
                pltpu.VMEM((total + 1, comps, ca, rows, cols), f32),
                pltpu.VMEM((comps, rows, cols), f32),
                pltpu.VMEM((total + 1, comps, rows, cols), f32),
                pltpu.VMEM((total, nc, comps, rows, cols), f32),
                pltpu.VMEM((total + 1, len(groups), rows, cols), f32),
                pltpu.VMEM((total, len(groups), 2, rows, cols), f32),
                pltpu.SemaphoreType.DMA((total, nc)),
                pltpu.SemaphoreType.DMA((total, nc)),
                pltpu.SemaphoreType.DMA((total, len(groups), 4)),
                pltpu.SemaphoreType.DMA((total, len(groups), 4)),
                *[pltpu.VMEM((total + 1, 2, rim, cols), f32) for rim in rims],
                *[pltpu.VMEM((total, 2, rim, cols), f32) for rim in rims],
            ],
            compiler_params=pltpu.CompilerParams(
                collective_id=0, has_side_effects=True, vmem_limit_bytes=60 * 1024 * 1024),
        )(flow, inflow, outflow, wheel, offsets)

    return jax.shard_map(
        per_device,
        mesh=mesh,
        in_specs=placed,
        out_specs=P("row", None, None, "rad", "circ"),
        check_vma=False,
    )
```

```python
import functools

import jax
import jax.numpy as jnp
from jax import lax
from jax.experimental import pallas as pl
from jax.experimental.pallas import tpu as pltpu
from jax.sharding import PartitionSpec as P

GAMMA = 1.4
COURANT = 0.1
MESH = pl.DeviceIdType.MESH
STAGES = 3
CUT = 7


def layer_groups(ca):
    cut = min(1 + CUT, ca)
    return [g for g in ([0], list(range(1, cut)), list(range(cut, ca))) if g]


def primitives(q):
    inverse = 1.0 / q[0]
    vel = [q[1] * inverse, q[2] * inverse, q[3] * inverse]
    kinetic = 0.5 * (q[1] * vel[0] + q[2] * vel[1] + q[3] * vel[2])
    pressure = (GAMMA - 1.0) * (q[4] - kinetic)
    sound = jnp.sqrt(GAMMA * pressure * inverse)
    return vel, pressure, sound


def normal_flux(q, prim, k):
    vel, pressure, sound = prim
    v = vel[k]
    f = [q[1 + k], q[1] * v, q[2] * v, q[3] * v, (q[4] + pressure) * v]
    f[1 + k] = f[1 + k] + pressure
    return f, jnp.abs(v) + sound


def jump(speed_a, speed_b, left, right):
    s = jnp.maximum(speed_a, speed_b)
    return [s * (right[c] - left[c]) for c in range(5)]


def kernel(
    nc, nr, steps,
    flow_hbm, inflow_hbm, outflow_hbm, wheel_ref, offsets_ref,
    out_ref,
    flow_ref, ends, in_sem,
    state, far, gsend, grecv, csend, crecv, gs_sem, gr_sem, hs_sem, hr_sem, *rims,
):
    inputs = [
        pltpu.make_async_copy(src, dst, in_sem.at[i])
        for i, (src, dst) in enumerate(
            ((flow_hbm, flow_ref), (inflow_hbm, ends.at[0]), (outflow_hbm, ends.at[1])))
    ]
    for copy in inputs:
        copy.start()
    ca, rows, cols = state.shape[2:]
    total = steps * STAGES
    row = lax.axis_index("row")
    me = lax.axis_index("circ")
    rad = lax.axis_index("rad")
    is_rotor = row == 0
    groups = layer_groups(ca)
    rsends, rrecvs = rims[: len(groups)], rims[len(groups) :]
    other = 1 - row
    right, left = lax.rem(me + 1, nc), lax.rem(me + nc - 1, nc)
    above, below = lax.rem(rad + 1, nr), lax.rem(rad + nr - 1, nr)

    barrier = pltpu.get_barrier_semaphore()
    for d in range(nc):
        pl.semaphore_signal(
            barrier, inc=1, device_id=(other, lax.rem(me + d, nc), rad), device_id_type=MESH)
    for peer in ((row, right, rad), (row, left, rad), (row, me, above), (row, me, below)):
        pl.semaphore_signal(barrier, inc=1, device_id=peer, device_id_type=MESH)

    lane = lax.broadcasted_iota(jnp.int32, (rows, cols), 1)
    sub = lax.broadcasted_iota(jnp.int32, (rows, cols), 0)
    first_lane, last_lane = lane == 0, lane == cols - 1
    first_sub, last_sub = sub == 0, sub == rows - 1
    wall_lo = jnp.logical_and(first_sub, rad == 0)
    wall_hi = jnp.logical_and(last_sub, rad == nr - 1)
    pair = lax.div(lane, 2)
    even = lax.rem(lane, 2) == 0
    sigma = jnp.where(is_rotor, jnp.float32(-1.0), jnp.float32(1.0))
    blade = jnp.zeros((rows, cols), jnp.float32)
    for r in range(rows):
        blade = jnp.where(sub == r, wheel_ref[r], blade)

    def axial(k):
        return jnp.where(is_rotor, ca - 1 - k, k)

    def target(d):
        return lax.rem(me + d, nc)

    def gather_copy(slot, d):
        return pltpu.make_async_remote_copy(
            src_ref=gsend.at[slot], dst_ref=grecv.at[slot, me],
            send_sem=gs_sem.at[slot, d], recv_sem=gr_sem.at[slot, me],
            device_id=(other, target(d), rad), device_id_type=MESH)

    def gather_arrival(slot, j):
        return pltpu.make_async_remote_copy(
            src_ref=gsend.at[slot], dst_ref=grecv.at[slot, j],
            send_sem=gs_sem.at[slot, j], recv_sem=gr_sem.at[slot, j],
            device_id=(other, me, rad), device_id_type=MESH)

    def halo_copies(slot, g):
        plan = (
            (csend.at[slot, g], crecv.at[slot, g, 0], (row, right, rad)),
            (csend.at[slot, g], crecv.at[slot, g, 1], (row, left, rad)),
            (rsends[g].at[slot, 0], rrecvs[g].at[slot, 0], (row, me, above)),
            (rsends[g].at[slot, 1], rrecvs[g].at[slot, 1], (row, me, below)),
        )
        return [
            pltpu.make_async_remote_copy(
                src_ref=src, dst_ref=dst, send_sem=hs_sem.at[slot, g, i],
                recv_sem=hr_sem.at[slot, g, i], device_id=peer, device_id_type=MESH)
            for i, (src, dst, peer) in enumerate(plan)
        ]

    def start_halos(slot, g):
        for copy in halo_copies(slot, g):
            copy.start()

    def start_gather(slot):
        for d in range(nc):
            gather_copy(slot, d).start()

    def position(k, c):
        g = next(i for i, group in enumerate(groups) if k in group)
        return g, c * len(groups[g]) + groups[g].index(k)

    def pack(slot, k, q, packed):
        for c in range(5):
            g, place = position(k, c)
            rsends[g][slot, 0, place : place + 1, :] = q[c][rows - 1 : rows, :]
            rsends[g][slot, 1, place : place + 1, :] = q[c][0:1, :]
            packed = jnp.where(pair == place, pltpu.roll(q[c], 2 * place + 1, 1), packed)
        return packed

    zero = jnp.zeros((rows, cols), jnp.float32)
    for copy in inputs:
        copy.wait()
    for c in range(5):
        far[c] = jnp.where(is_rotor, ends[0, c], ends[1, c])
    for g, group in enumerate(groups):
        packed = zero
        for k in group:
            q = [flow_ref[0, c, axial(k)] for c in range(5)]
            for c in range(5):
                state[0, c, k] = q[c]
                if k == 0:
                    gsend[0, c] = q[c]
            packed = pack(0, k, q, packed)
        csend[0, g] = packed
    pl.semaphore_wait(barrier, nc + 4)
    start_gather(0)
    for g in list(range(1, len(groups))) + [0]:
        start_halos(0, g)

    def stage(s, carry):
        step = lax.div(s, STAGES)
        phase = s - step * STAGES
        base = step * STAGES
        keep = jnp.where(phase == 0, 0.0, jnp.where(phase == 1, 0.75, 1.0 / 3.0)).astype(jnp.float32)
        mix = jnp.where(phase == 0, 1.0, jnp.where(phase == 1, 0.25, 2.0 / 3.0)).astype(jnp.float32)

        def halos(g):
            for copy in halo_copies(s, g):
                copy.wait_recv()
            return jnp.where(
                even, pltpu.roll(crecv[s, g, 1], cols - 1, 1), pltpu.roll(crecv[s, g, 0], 1, 1))

        def send(g, packed):
            csend[s + 1, g] = packed

            @pl.when(s < total - 1)
            def _():
                start_halos(s + 1, g)

        def load(k):
            q = [state[s, c, k] for c in range(5)]
            prim = primitives(q)
            f, speed = normal_flux(q, prim, 0)
            return q, prim, f, speed

        def in_plane(k, q, prim, merged):
            _, _, sound = prim
            speed = jnp.abs(prim[0][1]) + sound
            up, down = [], []
            for c in range(5):
                mirror = -q[c] if c == 2 else q[c]
                g, place = position(k, c)
                rim = rrecvs[g]
                u = jnp.where(last_sub, rim[s, 1, place : place + 1, :], pltpu.roll(q[c], rows - 1, 0))
                d = jnp.where(first_sub, rim[s, 0, place : place + 1, :], pltpu.roll(q[c], 1, 0))
                up.append(jnp.where(wall_hi, mirror, u))
                down.append(jnp.where(wall_lo, mirror, d))
            fu, su = normal_flux(up, primitives(up), 1)
            fd, sd = normal_flux(down, primitives(down), 1)
            ju, jd = jump(speed, su, q, up), jump(sd, speed, down, q)
            acc = [(fu[c] - fd[c]) - (ju[c] - jd[c]) for c in range(5)]
            speed = jnp.abs(prim[0][2]) + sound
            after, before = [], []
            for c in range(5):
                _, place = position(k, c)
                edge = pltpu.roll(merged, cols - 1 - 2 * place, 1)
                after.append(jnp.where(last_lane, edge, pltpu.roll(q[c], cols - 1, 1)))
                before.append(jnp.where(first_lane, edge, pltpu.roll(q[c], 1, 1)))
            fa, sa = normal_flux(after, primitives(after), 2)
            fb, sb = normal_flux(before, primitives(before), 2)
            ja, jb = jump(speed, sa, q, after), jump(sb, speed, before, q)
            return [acc[c] + ((fa[c] - fb[c]) - (ja[c] - jb[c])) for c in range(5)]

        def finish(k, q, acc):
            new = []
            for c in range(5):
                advanced = q[c] + (-0.5 * COURANT) * acc[c]
                new.append(keep * state[base, c, k] + mix * advanced)
                state[s + 1, c, k] = new[c]
            return new

        q0, prim0, f0, s0 = load(0)
        here = load(1)
        j0 = jump(s0, here[3], q0, here[0])
        axial0 = [sigma * here[2][c] - j0[c] for c in range(5)]
        toward_f, toward_j = f0, j0
        for g in range(1, len(groups)):
            merged = halos(g)
            packed = zero
            for k in groups[g]:
                q, prim, f, speed = here
                if k + 1 < ca:
                    here = load(k + 1)
                else:
                    qf = [far[c] for c in range(5)]
                    pf = primitives(qf)
                    here = (qf, pf) + normal_flux(qf, pf, 0)
                j = jump(speed, here[3], q, here[0])
                acc = in_plane(k, q, prim, merged)
                acc = [
                    acc[c] + sigma * (here[2][c] - toward_f[c]) - (j[c] - toward_j[c])
                    for c in range(5)
                ]
                packed = pack(s + 1, k, finish(k, q, acc), packed)
                toward_f, toward_j = f, j
            send(g, packed)
        acc0 = in_plane(0, q0, prim0, halos(0))
        acc0 = [acc0[c] + axial0[c] for c in range(5)]

        offset = offsets_ref[step]
        cycle = nc * cols
        shift = jnp.where(is_rotor, offset, cycle - offset)
        start = lax.rem(me * cols + shift, cycle)
        block = lax.div(start, cols)
        turn = start - block * cols
        back = lax.rem(cols - turn, cols)
        following = lax.rem(block + 1, nc)
        for j in range(nc):
            gather_arrival(s, j).wait_recv()
        ghost = []
        want = jnp.where(lane >= turn, block, following)
        for c in range(5):
            both = grecv[s, 0, c]
            for j in range(1, nc):
                both = jnp.where(want == j, grecv[s, j, c], both)
            ghost.append(pltpu.roll(both, back, 1))
        swirl = ghost[3]
        ghost[4] = ghost[4] + sigma * swirl * blade + 0.5 * ghost[0] * blade * blade
        ghost[3] = swirl + sigma * ghost[0] * blade
        fg, sg = normal_flux(ghost, primitives(ghost), 0)
        jg = jump(sg, s0, ghost, q0)
        acc0 = [acc0[c] - sigma * fg[c] + jg[c] for c in range(5)]
        new = finish(0, q0, acc0)
        for c in range(5):
            gsend[s + 1, c] = new[c]

        csend[s + 1, 0] = pack(s + 1, 0, new, zero)

        @pl.when(s < total - 1)
        def _():
            copies = halo_copies(s + 1, 0)
            for copy in copies:
                copy.start()
            start_gather(s + 1)

        return carry

    lax.fori_loop(0, total, stage, 0)
    for k in range(ca):
        for c in range(5):
            out_ref[0, c, axial(k)] = state[total, c, k]

    def drain(s, carry):
        for d in range(nc):
            gather_copy(s, d).wait_send()
        for g in range(len(groups)):
            for copy in halo_copies(s, g):
                copy.wait_send()
        return carry

    lax.fori_loop(0, total, drain, 0)


def solution(mesh):
    placed = (
        P("row", None, None, "rad", "circ"),
        P(None, "rad", "circ"),
        P(None, "rad", "circ"),
        P("rad"),
        P(),
    )
    nc, nr = mesh.shape["circ"], mesh.shape["rad"]

    def per_device(flow, inflow, outflow, wheel, offsets):
        _, comps, ca, rows, cols = flow.shape
        steps = offsets.shape[0]
        total = steps * STAGES
        vmem = pl.BlockSpec(memory_space=pltpu.VMEM)
        smem = pl.BlockSpec(memory_space=pltpu.SMEM)
        hbm = pl.BlockSpec(memory_space=pltpu.HBM)
        f32 = jnp.float32
        groups = layer_groups(ca)
        rims = [-(-comps * len(group) // 8) * 8 for group in groups]
        return pl.pallas_call(
            functools.partial(kernel, nc, nr, steps),
            out_shape=jax.ShapeDtypeStruct(flow.shape, f32),
            in_specs=[hbm, hbm, hbm, smem, smem],
            out_specs=vmem,
            scratch_shapes=[
                pltpu.VMEM(flow.shape, f32),
                pltpu.VMEM((2, comps, rows, cols), f32),
                pltpu.SemaphoreType.DMA((3,)),
                pltpu.VMEM((total + 1, comps, ca, rows, cols), f32),
                pltpu.VMEM((comps, rows, cols), f32),
                pltpu.VMEM((total + 1, comps, rows, cols), f32),
                pltpu.VMEM((total, nc, comps, rows, cols), f32),
                pltpu.VMEM((total + 1, len(groups), rows, cols), f32),
                pltpu.VMEM((total, len(groups), 2, rows, cols), f32),
                pltpu.SemaphoreType.DMA((total, nc)),
                pltpu.SemaphoreType.DMA((total, nc)),
                pltpu.SemaphoreType.DMA((total, len(groups), 4)),
                pltpu.SemaphoreType.DMA((total, len(groups), 4)),
                *[pltpu.VMEM((total + 1, 2, rim, cols), f32) for rim in rims],
                *[pltpu.VMEM((total, 2, rim, cols), f32) for rim in rims],
            ],
            compiler_params=pltpu.CompilerParams(
                collective_id=0, has_side_effects=True, vmem_limit_bytes=60 * 1024 * 1024),
        )(flow, inflow, outflow, wheel, offsets)

    return jax.shard_map(
        per_device,
        mesh=mesh,
        in_specs=placed,
        out_specs=P("row", None, None, "rad", "circ"),
        check_vma=False,
    )
```
